32 devices in a mesh: dp: 2 (over x), row: 4 (over z), col: 4 (over y, core).
Axes of the slice: x: 2, y: 2, z: 4, core: 2. Of those that a mesh axis runs over, the one named last changes fastest.
Arguments:
- activations: bfloat16 [9232, 1024], P(('dp', 'col'), 'row'), may hold values from -6 to 6
- first_gain: float32 [1024], P('row'), may hold values from 0.5 to 1.5
- first_shift: float32 [1024], P('row'), may hold values from -1.75 to 1.75
- joined_weight: bfloat16 [1024, 3072], P('row', 'col'), may hold values from -0.25 to 0.25
- query_bias: float32 [1024], P('col'), may hold values from -3 to 3
- value_bias: float32 [1024], P('col'), may hold values from -3 to 3
- output_weight: bfloat16 [1024, 1024], P('col', 'row'), may hold values from -0.75 to 0.75
- output_bias: float32 [1024], P('row'), may hold values from -3 to 3
- second_gain: float32 [1024], P('row'), may hold values from 0.5 to 1.5
- second_shift: float32 [1024], P('row'), may hold values from -1.75 to 1.75
- hidden_weight: bfloat16 [1024, 4096], P('row', 'col'), may hold values from -0.1875 to 0.1875
- hidden_bias: float32 [4096], P('col'), may hold values from -3 to 3
- return_weight: bfloat16 [4096, 1024], P('col', 'row'), may hold values from -0.09375 to 0.09375
- return_bias: float32 [1024], P('row'), may hold values from -3 to 3
- layer_grad: bfloat16 [9232, 1024], P(('dp', 'col'), 'row'), may hold values from -6 to 6
Outputs:
- layer_output: bfloat16 [9232, 1024], P(('dp', 'col'), 'row')
- input_grad: float32 [9232, 1024], P(('dp', 'col'), 'row')
- first_gain_grad: float32 [1024], P('row')
- first_shift_grad: float32 [1024], P('row')
- joined_weight_grad: float32 [1024, 3072], P('row', 'col')
- query_bias_grad: float32 [1024], P('col')
- value_bias_grad: float32 [1024], P('col')
- output_weight_grad: float32 [1024, 1024], P('col', 'row')
- output_bias_grad: float32 [1024], P('row')
- second_gain_grad: float32 [1024], P('row')
- second_shift_grad: float32 [1024], P('row')
- hidden_weight_grad: float32 [1024, 4096], P('row', 'col')
- hidden_bias_grad: float32 [4096], P('col')
- return_weight_grad: float32 [4096, 1024], P('col', 'row')
- return_bias_grad: float32 [1024], P('row')
The draws below stay inside these ranges and needn't reach their ends.
All inputs are finite; a program needn't handle non-finite values.
Results may differ from the reference program's by a relative error of at most 0.012.
The reference program's roundings to bfloat16 on the way count: a program that leaves them out, or rounds other values in their place, can miss the bound.
Values may be sent and summed in bfloat16 or wider, within the bound.
A program may use at most 128 MiB of HBM per device.

```python
import jax
import jax.numpy as jnp
from jax import lax

D = 1024
HEADS = 16
HEAD_DIM = 64
FF = 4096
SEQ = 577
TOKENS = 9232


def steps_of(own_key, dims, shards, least, largest):
    factor_of, own = 1.0, jax.random.fold_in(own_key, 6)
    for axis_at, blocks in shards:
        steps = jnp.exp(jax.random.uniform(jax.random.fold_in(own, axis_at), (blocks,), jnp.float32, least / len(shards), largest / len(shards)))
        factor_of = factor_of * jnp.repeat(steps, dims[axis_at] // blocks).reshape([-1 if axis == axis_at else 1 for axis in range(len(dims))])
    return factor_of


def centred(key, extent, deviation, most, cuts=(), dtype=jnp.bfloat16):
    level = steps_of(key, extent, cuts, -0.22, 0.18) if cuts else 1.0
    values = jax.random.normal(key, extent, jnp.float32) * deviation * level
    return jnp.minimum(jnp.maximum(values, -most), most).astype(dtype)


def setup_inputs(seed: int = 0) -> dict:
    keys = jax.random.split(jax.random.key(seed), 16)
    return {
        "activations": centred(keys[0], (TOKENS, D), 1.0, 6.0, ((0, 8), (1, 4))),
        "first_gain": jnp.clip(1.0 + 0.1 * jax.random.normal(keys[1], (D,), jnp.float32), 0.5, 1.5),
        "first_shift": centred(keys[2], (D,), 0.3, 1.75, ((0, 4),), jnp.float32),
        "joined_weight": centred(keys[3], (D, 3 * D), (D // 2) ** -0.5, 0.25, ((0, 4), (1, 4))),
        "query_bias": centred(keys[4], (D,), 0.5, 3.0, ((0, 4),), jnp.float32),
        "value_bias": centred(keys[5], (D,), 0.5, 3.0, ((0, 4),), jnp.float32),
        "output_weight": centred(keys[6], (D, D), (D // 16) ** -0.5, 0.75, ((0, 4), (1, 4))),
        "output_bias": centred(keys[7], (D,), 0.5, 3.0, ((0, 4),), jnp.float32),
        "second_gain": jnp.clip(1.0 + 0.1 * jax.random.normal(keys[8], (D,), jnp.float32), 0.5, 1.5),
        "second_shift": centred(keys[9], (D,), 0.3, 1.75, ((0, 4),), jnp.float32),
        "hidden_weight": centred(keys[10], (D, FF), D ** -0.5, 0.1875, ((0, 4), (1, 4))),
        "hidden_bias": centred(keys[11], (FF,), 0.5, 3.0, ((0, 4),), jnp.float32),
        "return_weight": centred(keys[12], (FF, D), FF ** -0.5, 0.09375, ((0, 4), (1, 4))),
        "return_bias": centred(keys[13], (D,), 0.5, 3.0, ((0, 4),), jnp.float32),
        "layer_grad": centred(keys[14], (TOKENS, D), 1.0, 6.0, ((0, 8), (1, 4))),
    }


EPSILON = 1e-06
HIGHEST_MODE = lax.Precision.HIGHEST

@jax.custom_vjp
def low(v):
    return lax.optimization_barrier(v.astype(jnp.bfloat16)).astype(jnp.float32)

@jax.custom_vjp
def low_back(v):
    return v

def low_keep(v):
    return (low(v), None)

def low_pass(kept, grad):
    return (grad,)

def back_keep(v):
    return (v, None)

def back_low(kept, grad):
    return (low(grad),)
low.defvjp(low_keep, low_pass)
low_back.defvjp(back_keep, back_low)

def matmul(left, right):
    return jnp.dot(left, right, precision=HIGHEST_MODE)

def layer_norm(values_in, norm_gain, norm_shift):
    center = lax.optimization_barrier(jnp.mean(values_in, axis=-1, keepdims=True))
    spread = lax.optimization_barrier(jnp.mean(values_in * values_in, axis=-1, keepdims=True)) - center * center
    return (values_in - center) * lax.rsqrt(spread + EPSILON) * norm_gain + norm_shift

def attend_image(image_block):
    query_rows = image_block[:, :, 0]
    key_rows = image_block[:, :, 1]
    value_rows = image_block[:, :, 2]
    scores = low_back(jnp.einsum('qhd,khd->hqk', query_rows, key_rows, precision=HIGHEST_MODE) * HEAD_DIM ** (-0.5))
    weights_soft = jax.nn.softmax(scores, axis=-1)
    return jnp.einsum('hqk,khd->qhd', low(weights_soft), value_rows, precision=HIGHEST_MODE)

def forward(activations, first_gain, first_shift, joined_weight, query_bias, value_bias, output_weight, output_bias, second_gain, second_shift, hidden_weight, hidden_bias, return_weight, return_bias):
    first_normed = low(layer_norm(activations, first_gain, first_shift))
    zero_part = jnp.zeros((HEADS, HEAD_DIM), jnp.float32)
    joined_bias = jnp.stack([query_bias.reshape(HEADS, HEAD_DIM), zero_part, value_bias.reshape(HEADS, HEAD_DIM)], axis=1).reshape(3 * D)
    joined = low(low_back(matmul(first_normed, joined_weight) + joined_bias))
    blocks = joined.reshape(-1, SEQ, HEADS, 3, HEAD_DIM)
    attended = lax.map(jax.checkpoint(attend_image), blocks)
    attended = low(low_back(attended.reshape(-1, D)))
    branch = low_back(matmul(attended, output_weight) + output_bias)
    hidden_in = activations + branch
    second_normed = low(layer_norm(hidden_in, second_gain, second_shift))
    pre_act = low_back(matmul(second_normed, hidden_weight) + hidden_bias)
    acted = low(jax.nn.gelu(pre_act, approximate=False))
    mixed = low_back(matmul(acted, return_weight) + return_bias)
    return hidden_in + mixed

def reference(activations, first_gain, first_shift, joined_weight, query_bias, value_bias, output_weight, output_bias, second_gain, second_shift, hidden_weight, hidden_bias, return_weight, return_bias, layer_grad):
    result, pullback = jax.vjp(forward, activations.astype(jnp.float32), first_gain, first_shift, joined_weight.astype(jnp.float32), query_bias, value_bias, output_weight.astype(jnp.float32), output_bias, second_gain, second_shift, hidden_weight.astype(jnp.float32), hidden_bias, return_weight.astype(jnp.float32), return_bias)
    input_grad, first_gain_grad, first_shift_grad, joined_weight_grad, query_bias_grad, value_bias_grad, output_weight_grad, output_bias_grad, second_gain_grad, second_shift_grad, hidden_weight_grad, hidden_bias_grad, return_weight_grad, return_bias_grad = pullback(layer_grad.astype(jnp.float32))
    return (result.astype(jnp.bfloat16), input_grad, first_gain_grad, first_shift_grad, joined_weight_grad, query_bias_grad, value_bias_grad, output_weight_grad, output_bias_grad, second_gain_grad, second_shift_grad, hidden_weight_grad, hidden_bias_grad, return_weight_grad, return_bias_grad)
```

```python
import math

import jax
import jax.numpy as jnp
from jax import lax
from jax.sharding import Mesh
from jax.sharding import PartitionSpec as P

D = 1024
HEAD_DIM = 64
SEQ = 577


EPSILON = 1e-06
ROOT_HALF = math.sqrt(0.5)
NORMAL_PEAK = 1.0 / math.sqrt(2.0 * math.pi)


def product(left, right):
    return jnp.dot(left, right, preferred_element_type=jnp.float32)


def over_rows(left, right):
    return lax.dot_general(
        left, right, (((0,), (0,)), ((), ())), preferred_element_type=jnp.float32
    )


def against_rows(left, right):
    return lax.dot_general(
        left, right, (((1,), (1,)), ((), ())), preferred_element_type=jnp.float32
    )


def swap_cores(piece):
    return lax.ppermute(piece, "core", [(0, 1), (1, 0)])


def core_sum(piece):
    return piece + swap_cores(piece)


def by_core(mine, other, axis):
    first = lax.axis_index("core") == 0
    return jnp.stack([jnp.where(first, mine, other), jnp.where(first, other, mine)], axis=axis)


def images_in(pieces):
    k = lax.axis_index("core")
    count, local, width = pieces.shape
    halves = pieces.reshape(count, local // SEQ, SEQ, 2, width // 2)
    mine = lax.dynamic_index_in_dim(halves, k, 3, keepdims=False)
    other = swap_cores(lax.dynamic_index_in_dim(halves, 1 - k, 3, keepdims=False))
    column = by_core(mine, other, 1).reshape(count, 2 * local // SEQ, SEQ, width // 2)
    chip = lax.all_to_all(column, "row", split_axis=1, concat_axis=3, tiled=True)
    rows = lax.axis_size("row")
    chip = chip.reshape(count, -1, rows, width // 2)
    return by_core(chip, swap_cores(chip), 3).reshape(count, -1, rows * width)


def images_out(values):
    k = lax.axis_index("core")
    rows = lax.axis_size("row")
    tokens, total = values.shape
    half = total // rows // 2
    mine = lax.dynamic_index_in_dim(values.reshape(tokens, rows, 2, half), k, 2, keepdims=False)
    mine = mine.reshape(tokens // SEQ, SEQ, rows * half)
    column = lax.all_to_all(mine, "row", split_axis=2, concat_axis=0, tiled=True)
    column = column.reshape(2, -1, half)
    kept = lax.dynamic_index_in_dim(column, k, 0, keepdims=False)
    other = swap_cores(lax.dynamic_index_in_dim(column, 1 - k, 0, keepdims=False))
    return by_core(kept, other, 1).reshape(-1, 2 * half)


def gather_blocks(block, split_columns):
    rows, pair = lax.axis_size("row"), lax.axis_size("y")
    high, wide = block.shape
    found = lax.all_gather(block, ("row", "y")).reshape(rows, pair, high, wide)
    if split_columns:
        return jnp.transpose(found, (1, 2, 0, 3)).reshape(pair * high, rows * wide)
    return jnp.transpose(found, (0, 2, 1, 3)).reshape(rows * high, pair * wide)


def scatter_blocks(grad, split_columns):
    rows, pair = lax.axis_size("row"), lax.axis_size("y")
    grad = grad.astype(jnp.bfloat16)
    high, wide = grad.shape
    if split_columns:
        parts = jnp.transpose(grad.reshape(pair, high // pair, rows, wide // rows), (2, 0, 1, 3))
    else:
        parts = jnp.transpose(grad.reshape(rows, high // rows, pair, wide // pair), (0, 2, 1, 3))
    parts = parts.reshape(rows * pair, *parts.shape[2:])
    share = lax.psum_scatter(parts, ("row", "y"), scatter_dimension=0)
    if lax.axis_size("dp") == 2:
        other = lax.ppermute(share, "dp", [(0, 1), (1, 0)])
        return share.astype(jnp.float32) + other.astype(jnp.float32)
    return lax.psum(share, "dp").astype(jnp.float32)


def norm_forward(values_in, norm_gain, norm_shift):
    center = jnp.mean(values_in, axis=1, keepdims=True)
    spread = jnp.mean(values_in * values_in, axis=1, keepdims=True) - center * center
    inv_std = lax.rsqrt(spread + EPSILON)
    normed = (values_in - center) * inv_std
    return (normed, inv_std, normed * norm_gain + norm_shift)


def norm_backward(grad_in, normed, inv_std, norm_gain):
    scaled = grad_in * norm_gain
    total = jnp.mean(scaled, axis=1, keepdims=True)
    along = jnp.mean(scaled * normed, axis=1, keepdims=True)
    return inv_std * (scaled - total - normed * along)


def gelu_value(inputs):
    return inputs * (lax.erf(inputs * ROOT_HALF) + 1.0) / 2.0


def gelu_slope(inputs):
    return (
        0.5 * (1.0 + lax.erf(inputs * ROOT_HALF))
        + inputs * jnp.exp(-0.5 * inputs * inputs) * NORMAL_PEAK
    )


def attend_forward(image_block):
    query_rows = image_block[0]
    key_rows = image_block[1]
    value_rows = image_block[2]
    scores = against_rows(query_rows, key_rows) * HEAD_DIM ** (-0.5)
    row_max = jnp.max(scores, axis=1, keepdims=True)
    raised = jnp.exp(scores - row_max)
    row_sum = jnp.sum(raised, axis=1, keepdims=True)
    weights_soft = raised / row_sum
    result = product(weights_soft.astype(jnp.bfloat16), value_rows)
    return (result, (row_max + jnp.log(row_sum))[:, 0])


def attend_backward(image_items):
    image_block, grad_rows, log_total = image_items
    query_rows = image_block[0]
    key_rows = image_block[1]
    value_rows = image_block[2]
    attn_scale = HEAD_DIM ** (-0.5)
    scores = against_rows(query_rows, key_rows) * attn_scale
    weights_soft = jnp.exp(scores - log_total[:, None])
    grad_weights = against_rows(grad_rows, value_rows)
    delta_rows = jnp.sum(grad_weights * weights_soft, axis=1, keepdims=True)
    grad_scores = (weights_soft * (grad_weights - delta_rows)).astype(jnp.bfloat16)
    grad_query = product(grad_scores, key_rows) * attn_scale
    grad_key = over_rows(grad_scores, query_rows) * attn_scale
    grad_value = over_rows(weights_soft.astype(jnp.bfloat16), grad_rows)
    return jnp.stack([grad_query, grad_key, grad_value], axis=0)


def body(
    activations,
    first_gain,
    first_shift,
    joined_weight,
    query_bias,
    value_bias,
    output_weight,
    output_bias,
    second_gain,
    second_shift,
    hidden_weight,
    hidden_bias,
    return_weight,
    return_bias,
    layer_grad,
):
    k = lax.axis_index("core")
    rows = lax.axis_size("row")
    pair = lax.axis_size("y")
    width = activations.shape[1]
    chip_images = 2 * activations.shape[0] // SEQ // rows
    tokens = chip_images * SEQ
    block_heads = query_bias.shape[0] // HEAD_DIM
    heads = pair * block_heads

    joined_all = gather_blocks(joined_weight, False)
    small_all = lax.all_gather(
        jnp.concatenate(
            [
                first_gain,
                first_shift,
                output_bias,
                second_gain,
                second_shift,
                return_bias,
                query_bias,
                value_bias,
                hidden_bias,
            ]
        ),
        ("row", "y"),
    ).reshape(rows, pair, -1)
    wide = small_all[:, 0, : 6 * width].reshape(rows, 6, width)
    wide = jnp.transpose(wide, (1, 0, 2)).reshape(6, -1)
    gain_one, shift_one, out_bias, gain_two, shift_two, ret_bias = (wide[i] for i in range(6))
    deep = small_all[0, :, 6 * width :]
    cut = query_bias.shape[0]
    q_bias = deep[:, :cut].reshape(heads, HEAD_DIM)
    v_bias = deep[:, cut : 2 * cut].reshape(heads, HEAD_DIM)
    h_bias = deep[:, 2 * cut :].reshape(-1)
    joined_bias = jnp.stack([q_bias, jnp.zeros_like(q_bias), v_bias], axis=1).reshape(-1)

    resid, layer_g = images_in(jnp.stack([activations, layer_grad]))
    output_all = gather_blocks(output_weight, True)
    hidden_all = gather_blocks(hidden_weight, False)
    return_all = gather_blocks(return_weight, True)
    resid = resid.astype(jnp.float32)
    normed_one, inv_one, first_out = norm_forward(resid, gain_one, shift_one)
    first_out = first_out.astype(jnp.bfloat16)
    joined = (product(first_out, joined_all) + joined_bias).astype(jnp.bfloat16)
    blocks = jnp.transpose(
        joined.reshape(chip_images, SEQ, heads, 3, HEAD_DIM), (0, 2, 3, 1, 4)
    ).reshape(-1, 3, SEQ, HEAD_DIM)
    attended, log_total = lax.map(attend_forward, blocks)
    attended = jnp.transpose(
        attended.astype(jnp.bfloat16).reshape(chip_images, heads, SEQ, HEAD_DIM), (0, 2, 1, 3)
    ).reshape(tokens, -1)
    branch = core_sum(product(attended, output_all)) + out_bias
    hidden_in = resid + branch
    normed_two, inv_two, second_out = norm_forward(hidden_in, gain_two, shift_two)
    second_out = second_out.astype(jnp.bfloat16)
    pre_act = product(second_out, hidden_all) + h_bias
    acted = gelu_value(pre_act).astype(jnp.bfloat16)
    mixed = core_sum(product(acted, return_all)) + ret_bias
    layer_output = images_out((hidden_in + mixed).astype(jnp.bfloat16))

    grad_out = layer_g.astype(jnp.float32)
    return_weight_grad = scatter_blocks(over_rows(acted, layer_g), True)
    grad_acted = against_rows(layer_g, return_all)
    grad_pre = (grad_acted * gelu_slope(pre_act)).astype(jnp.bfloat16)
    hidden_weight_grad = scatter_blocks(over_rows(second_out, grad_pre), False)
    grad_second = core_sum(against_rows(grad_pre, hidden_all))
    grad_hidden = grad_out + norm_backward(grad_second, normed_two, inv_two, gain_two)
    grad_branch = grad_hidden.astype(jnp.bfloat16)
    output_weight_grad = scatter_blocks(over_rows(attended, grad_branch), True)
    grad_attended = against_rows(grad_branch, output_all).astype(jnp.bfloat16)
    grad_heads = jnp.transpose(
        grad_attended.reshape(chip_images, SEQ, heads, HEAD_DIM), (0, 2, 1, 3)
    ).reshape(-1, SEQ, HEAD_DIM)
    grad_blocks = lax.map(attend_backward, (blocks, grad_heads, log_total))
    grad_joined = jnp.transpose(
        grad_blocks.astype(jnp.bfloat16).reshape(chip_images, heads, 3, SEQ, HEAD_DIM),
        (0, 3, 1, 2, 4),
    ).reshape(tokens, -1)
    joined_weight_grad = scatter_blocks(over_rows(first_out, grad_joined), False)
    grad_first = core_sum(against_rows(grad_joined, joined_all))
    input_grad = images_out(
        (grad_hidden + norm_backward(grad_first, normed_one, inv_one, gain_one)).astype(
            jnp.bfloat16
        )
    ).astype(jnp.float32)

    joined_terms = jnp.sum(grad_joined, axis=0, dtype=jnp.float32).reshape(
        pair, block_heads, 3, HEAD_DIM
    )
    wide_sums = jnp.stack(
        [
            jnp.sum(grad_first * normed_one, axis=0),
            jnp.sum(grad_first, axis=0),
            jnp.sum(grad_branch, axis=0, dtype=jnp.float32),
            jnp.sum(grad_second * normed_two, axis=0),
            jnp.sum(grad_second, axis=0),
            jnp.sum(grad_out, axis=0),
        ]
    )
    deep_sums = jnp.concatenate(
        [
            joined_terms[:, :, 0].reshape(pair, -1),
            joined_terms[:, :, 2].reshape(pair, -1),
            jnp.sum(grad_pre, axis=0, dtype=jnp.float32).reshape(pair, -1),
        ],
        axis=1,
    )
    sums = lax.psum(
        jnp.concatenate([wide_sums.reshape(-1), deep_sums.reshape(-1)]), ("dp", "row", "y")
    )
    wide_sums = sums[: wide_sums.size].reshape(6, rows, width)
    deep_sums = sums[wide_sums.size :].reshape(pair, -1)
    wide_sums = lax.dynamic_index_in_dim(wide_sums, lax.axis_index("row"), 1, keepdims=False)
    deep_sums = lax.dynamic_index_in_dim(deep_sums, lax.axis_index("y"), 0, keepdims=False)
    (
        first_gain_grad,
        first_shift_grad,
        output_bias_grad,
        second_gain_grad,
        second_shift_grad,
        return_bias_grad,
    ) = (wide_sums[i] for i in range(6))
    query_bias_grad = deep_sums[:cut]
    value_bias_grad = deep_sums[cut : 2 * cut]
    hidden_bias_grad = deep_sums[2 * cut :]
    return (
        layer_output,
        input_grad,
        first_gain_grad,
        first_shift_grad,
        joined_weight_grad,
        query_bias_grad,
        value_bias_grad,
        output_weight_grad,
        output_bias_grad,
        second_gain_grad,
        second_shift_grad,
        hidden_weight_grad,
        hidden_bias_grad,
        return_weight_grad,
        return_bias_grad,
    )


def solution(mesh):
    shape = mesh.shape
    mesh = Mesh(
        mesh.devices.reshape(shape["dp"], shape["row"], shape["col"] // 2, 2),
        ("dp", "row", "y", "core"),
    )
    in_specs = (
        P(("dp", "y", "core"), "row"),
        P("row"),
        P("row"),
        P("row", ("y", "core")),
        P(("y", "core")),
        P(("y", "core")),
        P(("y", "core"), "row"),
        P("row"),
        P("row"),
        P("row"),
        P("row", ("y", "core")),
        P(("y", "core")),
        P(("y", "core"), "row"),
        P("row"),
        P(("dp", "y", "core"), "row"),
    )
    out_specs = (
        P(("dp", "y", "core"), "row"),
        P(("dp", "y", "core"), "row"),
        P("row"),
        P("row"),
        P("row", ("y", "core")),
        P(("y", "core")),
        P(("y", "core")),
        P(("y", "core"), "row"),
        P("row"),
        P("row"),
        P("row"),
        P("row", ("y", "core")),
        P(("y", "core")),
        P(("y", "core"), "row"),
        P("row"),
    )
    return jax.shard_map(body, mesh=mesh, in_specs=in_specs, out_specs=out_specs, check_vma=False)
```

```python
import math

import jax
import jax.numpy as jnp
from jax import lax
from jax.sharding import Mesh
from jax.sharding import PartitionSpec as P

D = 1024
HEAD_DIM = 64
SEQ = 577


EPSILON = 1e-06
ROOT_HALF = math.sqrt(0.5)
NORMAL_PEAK = 1.0 / math.sqrt(2.0 * math.pi)


def product(left, right):
    return jnp.dot(left, right, preferred_element_type=jnp.float32)


def over_rows(left, right):
    return lax.dot_general(
        left, right, (((0,), (0,)), ((), ())), preferred_element_type=jnp.float32
    )


def against_rows(left, right):
    return lax.dot_general(
        left, right, (((1,), (1,)), ((), ())), preferred_element_type=jnp.float32
    )


def swap_cores(piece):
    return lax.ppermute(piece, "core", [(0, 1), (1, 0)])


def core_sum(piece):
    return piece + swap_cores(piece)


def by_core(mine, other, axis):
    first = lax.axis_index("core") == 0
    return jnp.stack([jnp.where(first, mine, other), jnp.where(first, other, mine)], axis=axis)


def images_in(pieces):
    k = lax.axis_index("core")
    count, local, width = pieces.shape
    halves = pieces.reshape(count, local // SEQ, SEQ, 2, width // 2)
    mine = lax.dynamic_index_in_dim(halves, k, 3, keepdims=False)
    other = swap_cores(lax.dynamic_index_in_dim(halves, 1 - k, 3, keepdims=False))
    column = by_core(mine, other, 1).reshape(count, 2 * local // SEQ, SEQ, width // 2)
    chip = lax.all_to_all(column, "row", split_axis=1, concat_axis=3, tiled=True)
    rows = lax.axis_size("row")
    chip = chip.reshape(count, -1, rows, width // 2)
    return by_core(chip, swap_cores(chip), 3).reshape(count, -1, rows * width)


def images_out(values):
    k = lax.axis_index("core")
    rows = lax.axis_size("row")
    tokens, total = values.shape
    half = total // rows // 2
    mine = lax.dynamic_index_in_dim(values.reshape(tokens, rows, 2, half), k, 2, keepdims=False)
    mine = mine.reshape(tokens // SEQ, SEQ, rows * half)
    column = lax.all_to_all(mine, "row", split_axis=2, concat_axis=0, tiled=True)
    column = column.reshape(2, -1, half)
    kept = lax.dynamic_index_in_dim(column, k, 0, keepdims=False)
    other = swap_cores(lax.dynamic_index_in_dim(column, 1 - k, 0, keepdims=False))
    return by_core(kept, other, 1).reshape(-1, 2 * half)


def swap_sides(piece):
    return lax.ppermute(piece, "side", [(0, 1), (1, 0)])


def by_side(mine, other, axis):
    first = lax.axis_index("side") == 0
    return jnp.stack([jnp.where(first, mine, other), jnp.where(first, other, mine)], axis=axis)


def gather_blocks(block, split_columns):
    rows, pair = lax.axis_size("row"), lax.axis_size("y")
    high, wide = block.shape
    half = lax.dynamic_index_in_dim(
        block.reshape(2, high // 2, wide), lax.axis_index("side"), 0, keepdims=False
    )
    found = lax.all_gather(half, ("row", "y"))
    found = by_side(found, swap_sides(found), 1).reshape(rows, pair, high, wide)
    if split_columns:
        return jnp.transpose(found, (1, 2, 0, 3)).reshape(pair * high, rows * wide)
    return jnp.transpose(found, (0, 2, 1, 3)).reshape(rows * high, pair * wide)


def share_halves(grad, split_columns):
    rows, pair = lax.axis_size("row"), lax.axis_size("y")
    side = lax.axis_index("side")
    grad = grad.astype(jnp.bfloat16)
    high, wide = grad.shape
    if split_columns:
        parts = grad.reshape(pair, 2, high // pair // 2, rows, wide // rows)
        order = (2, 0, 1, 3)
        mine = lax.dynamic_index_in_dim(parts, side, 1, keepdims=False)
        away = lax.dynamic_index_in_dim(parts, 1 - side, 1, keepdims=False)
    else:
        parts = grad.reshape(rows, 2, high // rows // 2, pair, wide // pair)
        order = (0, 2, 1, 3)
        mine = lax.dynamic_index_in_dim(parts, side, 1, keepdims=False)
        away = lax.dynamic_index_in_dim(parts, 1 - side, 1, keepdims=False)
    mine = jnp.transpose(mine, order)
    away = jnp.transpose(away, order)
    mine = mine.reshape(rows * pair, *mine.shape[2:])
    came = swap_sides(away.reshape(mine.shape))
    return (mine.astype(jnp.float32) + came.astype(jnp.float32)).astype(jnp.bfloat16)


def scatter_blocks(half):
    share = lax.psum_scatter(half, ("row", "y"), scatter_dimension=0)
    share = lax.psum(share, "far")
    whole = by_side(share, swap_sides(share), 0)
    return whole.reshape(-1, whole.shape[-1]).astype(jnp.float32)


def norm_forward(values_in, norm_gain, norm_shift):
    center = jnp.mean(values_in, axis=1, keepdims=True)
    spread = jnp.mean(values_in * values_in, axis=1, keepdims=True) - center * center
    inv_std = lax.rsqrt(spread + EPSILON)
    normed = (values_in - center) * inv_std
    return (normed, inv_std, normed * norm_gain + norm_shift)


def norm_backward(grad_in, normed, inv_std, norm_gain):
    scaled = grad_in * norm_gain
    total = jnp.mean(scaled, axis=1, keepdims=True)
    along = jnp.mean(scaled * normed, axis=1, keepdims=True)
    return inv_std * (scaled - total - normed * along)


def gelu_value(inputs):
    return inputs * (lax.erf(inputs * ROOT_HALF) + 1.0) / 2.0


def gelu_slope(inputs):
    return (
        0.5 * (1.0 + lax.erf(inputs * ROOT_HALF))
        + inputs * jnp.exp(-0.5 * inputs * inputs) * NORMAL_PEAK
    )


def attend_forward(image_block):
    query_rows = image_block[0]
    key_rows = image_block[1]
    value_rows = image_block[2]
    scores = against_rows(query_rows, key_rows) * HEAD_DIM ** (-0.5)
    row_max = jnp.max(scores, axis=1, keepdims=True)
    raised = jnp.exp(scores - row_max)
    row_sum = jnp.sum(raised, axis=1, keepdims=True)
    weights_soft = raised / row_sum
    result = product(weights_soft.astype(jnp.bfloat16), value_rows)
    return (result, (row_max + jnp.log(row_sum))[:, 0])


def attend_backward(image_items):
    image_block, grad_rows, log_total = image_items
    query_rows = image_block[0]
    key_rows = image_block[1]
    value_rows = image_block[2]
    attn_scale = HEAD_DIM ** (-0.5)
    scores = against_rows(query_rows, key_rows) * attn_scale
    weights_soft = jnp.exp(scores - log_total[:, None])
    grad_weights = against_rows(grad_rows, value_rows)
    delta_rows = jnp.sum(grad_weights * weights_soft, axis=1, keepdims=True)
    grad_scores = (weights_soft * (grad_weights - delta_rows)).astype(jnp.bfloat16)
    grad_query = product(grad_scores, key_rows) * attn_scale
    grad_key = over_rows(grad_scores, query_rows) * attn_scale
    grad_value = over_rows(weights_soft.astype(jnp.bfloat16), grad_rows)
    return jnp.stack([grad_query, grad_key, grad_value], axis=0)


def body(
    activations,
    first_gain,
    first_shift,
    joined_weight,
    query_bias,
    value_bias,
    output_weight,
    output_bias,
    second_gain,
    second_shift,
    hidden_weight,
    hidden_bias,
    return_weight,
    return_bias,
    layer_grad,
):
    k = lax.axis_index("core")
    rows = lax.axis_size("row")
    pair = lax.axis_size("y")
    width = activations.shape[1]
    chip_images = 2 * activations.shape[0] // SEQ // rows
    tokens = chip_images * SEQ
    block_heads = query_bias.shape[0] // HEAD_DIM
    heads = pair * block_heads

    small_all = lax.all_gather(
        jnp.concatenate(
            [
                first_gain,
                first_shift,
                output_bias,
                second_gain,
                second_shift,
                return_bias,
                query_bias,
                value_bias,
                hidden_bias,
            ]
        ),
        ("row", "y"),
    ).reshape(rows, pair, -1)
    joined_weight, small_all = lax.optimization_barrier((joined_weight, small_all))
    joined_all = gather_blocks(joined_weight, False)
    wide = small_all[:, 0, : 6 * width].reshape(rows, 6, width)
    wide = jnp.transpose(wide, (1, 0, 2)).reshape(6, -1)
    gain_one, shift_one, out_bias, gain_two, shift_two, ret_bias = (wide[i] for i in range(6))
    deep = small_all[0, :, 6 * width :]
    cut = query_bias.shape[0]
    q_bias = deep[:, :cut].reshape(heads, HEAD_DIM)
    v_bias = deep[:, cut : 2 * cut].reshape(heads, HEAD_DIM)
    h_bias = deep[:, 2 * cut :].reshape(-1)
    joined_bias = jnp.stack([q_bias, jnp.zeros_like(q_bias), v_bias], axis=1).reshape(-1)

    resid, layer_g = images_in(jnp.stack([activations, layer_grad]))
    output_weight, joined_all = lax.optimization_barrier((output_weight, joined_all))
    output_all = gather_blocks(output_weight, True)
    hidden_weight, output_all = lax.optimization_barrier((hidden_weight, output_all))
    hidden_all = gather_blocks(hidden_weight, False)
    return_all = gather_blocks(return_weight, True)
    resid = resid.astype(jnp.float32)
    normed_one, inv_one, first_out = norm_forward(resid, gain_one, shift_one)
    first_out = first_out.astype(jnp.bfloat16)
    joined = (product(first_out, joined_all) + joined_bias).astype(jnp.bfloat16)
    blocks = jnp.transpose(
        joined.reshape(chip_images, SEQ, heads, 3, HEAD_DIM), (0, 2, 3, 1, 4)
    ).reshape(-1, 3, SEQ, HEAD_DIM)
    attended, log_total = lax.map(attend_forward, blocks)
    attended = jnp.transpose(
        attended.astype(jnp.bfloat16).reshape(chip_images, heads, SEQ, HEAD_DIM), (0, 2, 1, 3)
    ).reshape(tokens, -1)
    branch = core_sum(product(attended, output_all)) + out_bias
    hidden_in = resid + branch
    normed_two, inv_two, second_out = norm_forward(hidden_in, gain_two, shift_two)
    second_out = second_out.astype(jnp.bfloat16)
    pre_act = product(second_out, hidden_all) + h_bias
    acted = gelu_value(pre_act).astype(jnp.bfloat16)
    mixed = core_sum(product(acted, return_all)) + ret_bias
    layer_output = images_out((hidden_in + mixed).astype(jnp.bfloat16))

    grad_out = layer_g.astype(jnp.float32)
    return_half = share_halves(over_rows(acted, layer_g), True)
    grad_acted = against_rows(layer_g, return_all)
    grad_pre = (grad_acted * gelu_slope(pre_act)).astype(jnp.bfloat16)
    hidden_half = share_halves(over_rows(second_out, grad_pre), False)
    grad_second = core_sum(against_rows(grad_pre, hidden_all))
    grad_second, return_half = lax.optimization_barrier((grad_second, return_half))
    return_weight_grad = scatter_blocks(return_half)
    grad_hidden = grad_out + norm_backward(grad_second, normed_two, inv_two, gain_two)
    grad_branch = grad_hidden.astype(jnp.bfloat16)
    output_half = share_halves(over_rows(attended, grad_branch), True)
    grad_attended = against_rows(grad_branch, output_all).astype(jnp.bfloat16)
    grad_heads = jnp.transpose(
        grad_attended.reshape(chip_images, SEQ, heads, HEAD_DIM), (0, 2, 1, 3)
    ).reshape(-1, SEQ, HEAD_DIM)
    grad_heads, hidden_half, output_half = lax.optimization_barrier(
        (grad_heads, hidden_half, output_half)
    )
    hidden_weight_grad = scatter_blocks(hidden_half)
    output_weight_grad = scatter_blocks(output_half)
    grad_blocks = lax.map(attend_backward, (blocks, grad_heads, log_total))
    grad_joined = jnp.transpose(
        grad_blocks.astype(jnp.bfloat16).reshape(chip_images, heads, 3, SEQ, HEAD_DIM),
        (0, 3, 1, 2, 4),
    ).reshape(tokens, -1)
    joined_weight_grad = scatter_blocks(share_halves(over_rows(first_out, grad_joined), False))
    grad_first = core_sum(against_rows(grad_joined, joined_all))
    input_grad = images_out(
        (grad_hidden + norm_backward(grad_first, normed_one, inv_one, gain_one)).astype(
            jnp.bfloat16
        )
    ).astype(jnp.float32)

    joined_terms = jnp.sum(grad_joined, axis=0, dtype=jnp.float32).reshape(
        pair, block_heads, 3, HEAD_DIM
    )
    wide_sums = jnp.stack(
        [
            jnp.sum(grad_first * normed_one, axis=0),
            jnp.sum(grad_first, axis=0),
            jnp.sum(grad_branch, axis=0, dtype=jnp.float32),
            jnp.sum(grad_second * normed_two, axis=0),
            jnp.sum(grad_second, axis=0),
            jnp.sum(grad_out, axis=0),
        ]
    )
    deep_sums = jnp.concatenate(
        [
            joined_terms[:, :, 0].reshape(pair, -1),
            joined_terms[:, :, 2].reshape(pair, -1),
            jnp.sum(grad_pre, axis=0, dtype=jnp.float32).reshape(pair, -1),
        ],
        axis=1,
    )
    sums = lax.psum(
        jnp.concatenate([wide_sums.reshape(-1), deep_sums.reshape(-1)]), ("far", "side", "row", "y")
    )
    wide_sums = sums[: wide_sums.size].reshape(6, rows, width)
    deep_sums = sums[wide_sums.size :].reshape(pair, -1)
    wide_sums = lax.dynamic_index_in_dim(wide_sums, lax.axis_index("row"), 1, keepdims=False)
    deep_sums = lax.dynamic_index_in_dim(deep_sums, lax.axis_index("y"), 0, keepdims=False)
    (
        first_gain_grad,
        first_shift_grad,
        output_bias_grad,
        second_gain_grad,
        second_shift_grad,
        return_bias_grad,
    ) = (wide_sums[i] for i in range(6))
    query_bias_grad = deep_sums[:cut]
    value_bias_grad = deep_sums[cut : 2 * cut]
    hidden_bias_grad = deep_sums[2 * cut :]
    return (
        layer_output,
        input_grad,
        first_gain_grad,
        first_shift_grad,
        joined_weight_grad,
        query_bias_grad,
        value_bias_grad,
        output_weight_grad,
        output_bias_grad,
        second_gain_grad,
        second_shift_grad,
        hidden_weight_grad,
        hidden_bias_grad,
        return_weight_grad,
        return_bias_grad,
    )


def solution(mesh):
    shape = mesh.shape
    mesh = Mesh(
        mesh.devices.reshape(shape["dp"] // 2, 2, shape["row"], shape["col"] // 2, 2),
        ("far", "side", "row", "y", "core"),
    )
    in_specs = (
        P(("far", "side", "y", "core"), "row"),
        P("row"),
        P("row"),
        P("row", ("y", "core")),
        P(("y", "core")),
        P(("y", "core")),
        P(("y", "core"), "row"),
        P("row"),
        P("row"),
        P("row"),
        P("row", ("y", "core")),
        P(("y", "core")),
        P(("y", "core"), "row"),
        P("row"),
        P(("far", "side", "y", "core"), "row"),
    )
    out_specs = (
        P(("far", "side", "y", "core"), "row"),
        P(("far", "side", "y", "core"), "row"),
        P("row"),
        P("row"),
        P("row", ("y", "core")),
        P(("y", "core")),
        P(("y", "core")),
        P(("y", "core"), "row"),
        P("row"),
        P("row"),
        P("row"),
        P("row", ("y", "core")),
        P(("y", "core")),
        P(("y", "core"), "row"),
        P("row"),
    )
    return jax.shard_map(body, mesh=mesh, in_specs=in_specs, out_specs=out_specs, check_vma=False)
```
